32 devices in a mesh: mem: 4 (over y, x), lon: 8 (over z, core).
Axes of the slice: x: 2, y: 2, z: 4, core: 2. Of those that a mesh axis runs over, the one named last changes fastest.
Arguments:
- members: float32 [16, 256, 12, 720], P('mem', 'lon'), may hold values from -6 to 6
- control: float32 [256, 12, 720], P('lon', None, 'mem'), may hold values from -6 to 6
- sea_mask: int32 [256, 12], P('lon'), may hold values 0 or 1
- depth_class: int32 [256, 12], P('lon'), may hold values from 0 to 3
- wind_dir: int32 [256, 12], P('lon'), may hold values from 0 to 23
- growth: float32 [30], replicated, may hold values from 0.2 to 2
- kernel: float32 [720, 720], replicated, may hold values from -0.21875 to 0.21875
Outputs:
- spectra: float32 [16, 256, 12, 720], P('mem', 'lon')
The draws below stay inside these ranges and needn't reach their ends.
All inputs are finite; a program needn't handle non-finite values. No bound on the sum of `sea_mask` on one device may be relied on, other than what follows from the above.
Results may differ from the reference program's by a relative error of at most 0.0001.
Values sent between devices are 32-bit elements; how exact they have to be, the bound alone decides.
A program may use at most 128 MiB of HBM per device.

```python
import math
import jax
import jax.numpy as jnp
from jax import lax

DIRS = 24
FREQS = 30
NLAT = 12
BINS = 720
MEMBERS = 16
NLON = 256


def place_ends(values, stream_key, low, largest):
    index_at = [jax.random.randint(jax.random.fold_in(stream_key, axis), (), 0, length) for axis, length in enumerate(values.shape)]
    longest = values.shape.index(max(values.shape))
    neighbour = index_at[:longest] + [(index_at[longest] + 1) % values.shape[longest]] + index_at[longest + 1:]
    return values.at[tuple(index_at)].set(low).at[tuple(neighbour)].set(largest)


def block_levels(own_key, dims, pieces, low, high):
    def one(position, shards_of):
        heights = jax.random.uniform(jax.random.fold_in(jax.random.fold_in(own_key, 6), position), (shards_of,), jnp.float32, low / len(pieces), high / len(pieces))
        return jnp.repeat(jnp.exp(heights), dims[position] // shards_of).reshape((-1,) + (1,) * (len(dims) - position - 1))

    factor_of = one(*pieces[0])
    for cut in pieces[1:]:
        factor_of = factor_of * one(*cut)
    return factor_of


def bell_draw(rng, dims, deviation, most, pieces=(), kind=jnp.bfloat16):
    values = deviation * jax.random.normal(rng, dims, jnp.float32)
    if pieces:
        values = values * block_levels(rng, dims, pieces, -0.22, 0.18)
    return jnp.clip(values, -most, most).astype(kind)


def setup_inputs(seed: int = 0) -> dict:
    arg_keys = jax.random.split(jax.random.key(seed), 8)
    members = bell_draw(arg_keys[0], (MEMBERS, NLON, NLAT, BINS), 1.0, 6.0, ((0, 4), (1, 8)), jnp.float32)
    control = bell_draw(arg_keys[1], (NLON, NLAT, BINS), 1.0, 6.0, ((0, 8), (2, 4)), jnp.float32)
    sea_mask = place_ends((jax.random.randint(arg_keys[2], (NLON, NLAT), 0, 5) < 4).astype(jnp.int32), jax.random.fold_in(arg_keys[2], 1), 0, 1)
    depth_class = place_ends(jax.random.randint(arg_keys[3], (NLON, NLAT), 0, 4), jax.random.fold_in(arg_keys[3], 1), 0, 3).astype(jnp.int32)
    wind_dir = place_ends(jax.random.randint(arg_keys[4], (NLON, NLAT), 0, DIRS), jax.random.fold_in(arg_keys[4], 1), 0, DIRS - 1).astype(jnp.int32)
    growth = jnp.clip(jnp.exp(jax.random.uniform(arg_keys[5], (FREQS,), jnp.float32, math.log(0.2), math.log(2.0))), 0.2, 2.0)
    kernel = bell_draw(arg_keys[6], (BINS, BINS), BINS ** -0.5, 0.21875, (), jnp.float32)
    return {"members": members, "control": control, "sea_mask": sea_mask, "depth_class": depth_class, "wind_dir": wind_dir, "growth": growth, "kernel": kernel}


def wave_tables(sea_mask, depth_class, wind_dir, growth):
    cells_lon, rows_lat = sea_mask.shape
    frequency = 0.04 * jnp.power(jnp.float32(1.1), jnp.arange(FREQS).astype(jnp.float32))
    deep_speed = 9.81 / (4.0 * math.pi * frequency)
    depths = jnp.array([10.0, 30.0, 80.0, 200.0], jnp.float32)
    shallow = jnp.sqrt(9.81 * depths)
    group_speed = jnp.minimum(deep_speed[None, :], shallow[:, None])
    fastest = 9.81 / (4.0 * math.pi * 0.04)
    onehot = (depth_class[..., None] == jnp.arange(4).astype(jnp.int32)).astype(jnp.float32)
    cell_speed = 0.7 * lax.optimization_barrier(jnp.sum(onehot[..., None] * group_speed, axis=2)) / fastest
    angles = 2.0 * math.pi * jnp.arange(DIRS).astype(jnp.float32) / DIRS
    zonal_speed = (cell_speed[:, :, None, :] * jnp.cos(angles)[:, None]).reshape(cells_lon, rows_lat, DIRS * FREQS)
    merid_speed = (cell_speed[:, :, None, :] * jnp.sin(angles)[:, None]).reshape(cells_lon, rows_lat, DIRS * FREQS)
    relative = (jnp.arange(DIRS).astype(jnp.int32)[None, None, :] - wind_dir[..., None]).astype(jnp.float32)
    alignment = jnp.maximum(jnp.cos(2.0 * math.pi * relative / DIRS), 0.0)
    wind_gain = (alignment[..., None] * growth[None, None, None, :]).reshape(cells_lon, rows_lat, DIRS * FREQS)
    ocean = sea_mask.astype(jnp.float32)[..., None]
    return (zonal_speed, merid_speed, wind_gain, ocean)

def advect(centre, west_side, east_side, zonal_speed, merid_speed):
    lat_pad = jnp.pad(centre, ((0, 0), (0, 0), (1, 1), (0, 0)))
    south_side = lat_pad[:, :, :-2]
    north_side = lat_pad[:, :, 2:]
    flux = jnp.maximum(zonal_speed, 0.0) * (centre - west_side) + jnp.minimum(zonal_speed, 0.0) * (east_side - centre)
    flux = flux + jnp.maximum(merid_speed, 0.0) * (centre - south_side) + jnp.minimum(merid_speed, 0.0) * (north_side - centre)
    return centre - flux

def source(field, wind_gain, ocean, kernel):
    energy = lax.optimization_barrier(jnp.mean(field * field, axis=-1, keepdims=True))
    shape = field.shape
    transfer = jnp.dot(field.reshape(-1, shape[-1]), kernel, precision=lax.Precision.HIGHEST, preferred_element_type=jnp.float32).reshape(shape)
    return (field + 0.1 * (wind_gain * field - 0.5 * energy * field + transfer)) * ocean

def reference(members, control, sea_mask, depth_class, wind_dir, growth, kernel):
    total = lax.optimization_barrier(jnp.sum(members, axis=0))
    zonal_speed, merid_speed, wind_gain, ocean = wave_tables(sea_mask, depth_class, wind_dir, growth)

    def one_member(member):
        field = ((member - total / MEMBERS + control) * ocean)[None]
        for repeat in range(2):
            west_side = jnp.roll(field, 1, axis=1)
            east_side = jnp.roll(field, -1, axis=1)
            moved = advect(field, west_side, east_side, zonal_speed, merid_speed)
            field = source(moved, wind_gain, ocean, kernel)
        return field[0]
    return lax.map(one_member, members)
```

```python
import functools
import math

import jax
import jax.numpy as jnp
import numpy as np
from jax import lax
from jax.experimental import pallas as pl
from jax.experimental.pallas import tpu as pltpu
from jax.sharding import PartitionSpec as P

DIRS = 24
FREQS = 30
LANES = 128
CLASSES = 4


def round_up(x, to):
    return -(-x // to) * to


def constants(bins, width):
    frequency = 0.04 * 1.1 ** np.arange(FREQS, dtype=np.float64)
    deep = 9.81 / (4.0 * math.pi * frequency)
    shallow = np.sqrt(9.81 * np.array([10.0, 30.0, 80.0, 200.0]))
    speed = 0.7 * np.minimum(deep[None], shallow[:, None]) / (9.81 / (4.0 * math.pi * 0.04))
    angles = 2.0 * math.pi * np.arange(DIRS) / DIRS
    cos, sin = np.cos(angles), np.sin(angles)
    cos[np.abs(cos) < 1e-9] = 0.0
    sin[np.abs(sin) < 1e-9] = 0.0
    lift = lambda v: (v[None, :, None] * speed[:, None, :]).reshape(CLASSES, bins)
    a, b = lift(np.abs(cos)), lift(np.abs(sin))
    tab = np.zeros((LANES, 3 * width), np.float32)
    tab[:CLASSES, :bins] = a
    tab[:CLASSES, width : width + bins] = b
    tab[:CLASSES, 2 * width : 2 * width + bins] = -(a + b)
    tab[CLASSES + DIRS, 2 * width : 2 * width + bins] = 1.0
    rel = np.arange(DIRS)[None, :] - np.arange(DIRS)[:, None]
    align = np.maximum(np.cos(2.0 * math.pi * rel / DIRS), 0.0)
    wind = np.zeros((LANES, width), np.float32)
    wind[CLASSES : CLASSES + DIRS, :bins] = 0.1 * np.repeat(align, FREQS, axis=1)
    one = np.zeros((LANES, width), np.float32)
    one[CLASSES + DIRS, :bins] = 1.0
    cs = np.zeros(width, np.int32)
    sn = np.zeros(width, np.int32)
    cs[:bins] = np.repeat(np.sign(cos), FREQS)
    sn[:bins] = np.repeat(np.sign(sin), FREQS)
    return tab, wind, one, cs, sn


def spans(sign):
    out = []
    for c in range(len(sign) // LANES):
        s = sign[c * LANES : (c + 1) * LANES]
        if (s >= 0).all():
            out.append(1)
        elif (s <= 0).all():
            out.append(-1)
        else:
            pos = np.nonzero(s > 0)[0]
            out.append((int(pos[0]), int(pos[-1]) + 1))
            assert (s[pos[0] : pos[-1] + 1] >= 0).all()
    return out


def kernel(
    n, lons, count, rows_lat, tile, bins, width, zspan, mspan, total_members,
    m_hbm, ctrl_hbm, k_hbm, oh_ref, tab_ref, wind_ref, one_ref, growth_ref,
    out_hbm,
    mv, ctrlv, kv, ctrlp, dl, rsb, dfull, f0, f1, ta, tb, tc, tw, rk, lhs, gbuf, ebuf,
    snd, rcv,
    m_sem, in_sem, out_sem, rs_s, rs_r, ag_s, ag_r, h_s, h_r,
):
    me = lax.axis_index("mem")
    at = lax.axis_index("lon")
    right = lax.rem(at + 1, lons)
    left = lax.rem(at + lons - 1, lons)
    cells = rows_lat * tile
    part = cells // n
    cols = width // LANES
    block = 3 if rows_lat % 3 == 0 else 1
    blocks = rows_lat // block
    own_bins = ctrlv.shape[1]

    def peer(o):
        return lax.rem(me + o, n)

    def rows_of(q):
        return pl.ds(pl.multiple_of(q * part, 8), part)

    def m_copy(o):
        r = rows_of(peer(o))
        return pltpu.make_async_copy(m_hbm.at[:, r], mv.at[:, r], m_sem.at[o])

    order = list(range(1, n)) + [0]
    c_copy = pltpu.make_async_copy(ctrl_hbm, ctrlv, in_sem.at[0])
    k_copy = pltpu.make_async_copy(k_hbm, kv, in_sem.at[1])
    c_copy.start()
    for o in order:
        m_copy(o).start()
    k_copy.start()

    barrier = pltpu.get_barrier_semaphore()
    for o in range(1, n):
        pl.semaphore_signal(barrier, inc=1, device_id={"mem": peer(o)}, device_id_type=pl.DeviceIdType.MESH)
    for side in (left, right):
        pl.semaphore_signal(barrier, inc=1, device_id={"lon": side}, device_id_type=pl.DeviceIdType.MESH)

    ctrlp[...] = jnp.zeros_like(ctrlp)
    c_copy.wait()
    for k in range(n):
        @pl.when(me == k)
        def _():
            ctrlp[:, k * own_bins : (k + 1) * own_bins] = ctrlv[...]

    pl.semaphore_wait(barrier, n + 1)

    def rs_copy(o):
        q = peer(o)
        return pltpu.make_async_remote_copy(
            src_ref=dl.at[rows_of(q)], dst_ref=rsb.at[o - 1], send_sem=rs_s.at[o - 1], recv_sem=rs_r.at[o - 1],
            device_id={"mem": q}, device_id_type=pl.DeviceIdType.MESH,
        )

    def ag_copy(o):
        r = rows_of(me)
        return pltpu.make_async_remote_copy(
            src_ref=dfull.at[r], dst_ref=dfull.at[r], send_sem=ag_s.at[o - 1], recv_sem=ag_r.at[o - 1],
            device_id={"mem": peer(o)}, device_id_type=pl.DeviceIdType.MESH,
        )

    def ag_arrival(o):
        r = rows_of(lax.rem(me + n - o, n))
        return pltpu.make_async_remote_copy(
            src_ref=dfull.at[r], dst_ref=dfull.at[r], send_sem=ag_s.at[o - 1], recv_sem=ag_r.at[o - 1],
            device_id={"mem": peer(o)}, device_id_type=pl.DeviceIdType.MESH,
        )

    step = 16 if part % 16 == 0 else 8
    for o in order:
        m_copy(o).wait()
        base = peer(o) * part

        @pl.loop(0, part // step)
        def _(i):
            r = pl.ds(pl.multiple_of(base + i * step, 8), step)
            s = mv[0, r, :]
            for m in range(1, count):
                s = s + mv[m, r, :]
            dl[r, :] = ctrlp[r, :] - s * (1.0 / total_members)

        if o:
            rs_copy(o).start()

    @pl.loop(0, rows_lat)
    def _(i):
        r = pl.ds(pl.multiple_of(i * tile, 8), tile)
        oh = oh_ref[r, :]
        hot = functools.partial(jnp.dot, oh, precision=lax.Precision.HIGHEST, preferred_element_type=jnp.float32)
        ta[r, :] = hot(tab_ref[:, :width])
        tb[r, :] = hot(tab_ref[:, width : 2 * width])
        tc[r, :] = hot(tab_ref[:, 2 * width :])
        tw[r, :] = hot(wind_ref[...] * growth_ref[...] + one_ref[...])

    rk[...] = jnp.zeros_like(rk)
    k_copy.wait()

    @pl.loop(0, bins // 16)
    def _(i):
        k = kv[pl.ds(pl.multiple_of(i * 16, 16), 16), :] * 0.1
        hi = k.astype(jnp.bfloat16)
        lo = (k - hi.astype(jnp.float32)).astype(jnp.bfloat16)
        rk[pl.ds(pl.multiple_of(i * 16, 16), 16), :bins] = hi
        rk[pl.ds(pl.multiple_of(width + i * 16, 16), 16), :bins] = hi
        rk[pl.ds(pl.multiple_of(2 * width + i * 16, 16), 16), :bins] = lo

    zero = jnp.zeros((tile, width), jnp.float32)
    for m in range(count):
        for f in (f0, f1):
            f[m, 0] = zero
            f[m, rows_lat + 1] = zero

        @pl.loop(0, rows_lat)
        def _(i):
            f0[m, i + 1, :, width - LANES :] = jnp.zeros((tile, LANES), jnp.float32)

    def halo_copies(sub, g):
        r = pl.ds(g * block, block)
        made = []
        for side, to in ((0, right), (1, left)):
            made.append(pltpu.make_async_remote_copy(
                src_ref=snd.at[sub, side, r], dst_ref=rcv.at[sub, side, r],
                send_sem=h_s.at[sub, side, g], recv_sem=h_r.at[sub, side, g],
                device_id={"lon": to}, device_id_type=pl.DeviceIdType.MESH,
            ))
        return made

    def keep_edges(sub, f, lat):
        snd[sub, 0, lat] = jnp.concatenate([f[m, lat + 1, tile - 1 : tile, :] for m in range(count)], axis=0)
        snd[sub, 1, lat] = jnp.concatenate([f[m, lat + 1, 0:1, :] for m in range(count)], axis=0)

    for o in range(1, n):
        rs_copy(o).wait_recv()

    @pl.loop(0, part // step)
    def _(i):
        r = pl.ds(pl.multiple_of(me * part + i * step, 8), step)
        s = dl[r, :]
        for o in range(1, n):
            s = s + rsb[o - 1, pl.ds(pl.multiple_of(i * step, 8), step), :]
        dfull[r, :] = s

    for o in range(1, n):
        ag_copy(o).start()

    def recentre(g):
        @pl.loop(0, block)
        def _(i):
            lat = g * block + i
            r = pl.ds(pl.multiple_of(lat * tile, 8), tile)
            sea = oh_ref[r, CLASSES + DIRS : CLASSES + DIRS + 1] > 0.5
            d = dfull[r, :]
            for m in range(count):
                f0[m, lat + 1, :, :bins] = jnp.where(sea, mv[m, r, :] + d, 0.0)
            keep_edges(0, f0, lat)
        for c in halo_copies(0, g):
            c.start()

    if blocks == n:
        for o in range(n):
            if o:
                ag_arrival(o).wait_recv()
            recentre(lax.rem(me + n - o, n))
    else:
        for o in range(1, n):
            ag_arrival(o).wait_recv()
        for g in range(blocks):
            recentre(g)

    row = lax.broadcasted_iota(jnp.int32, (tile, LANES), 0)
    lane = lax.broadcasted_iota(jnp.int32, (tile, LANES), 1)

    def pick(span, behind, ahead):
        if span == 1:
            return behind()
        if span == -1:
            return ahead()
        return jnp.where((lane >= span[0]) & (lane < span[1]), behind(), ahead())

    def substep(sub, f, write):
        @pl.loop(0, blocks)
        def _(g):
            for c in halo_copies(sub, g):
                c.wait_recv()

            @pl.loop(0, block)
            def _(i):
                lat = g * block + i
                r = pl.ds(pl.multiple_of(lat * tile, 8), tile)
                acc = [None] * count
                for c in range(cols):
                    l = slice(c * LANES, (c + 1) * LANES)
                    va, vb, vc = ta[r, l], tb[r, l], tc[r, l]
                    for m in range(count):
                        x = f[m, lat + 1, :, l]
                        west = lambda: jnp.where(row == 0, rcv[sub, 0, lat, m : m + 1, l], pltpu.roll(x, 1, 0))
                        east = lambda: jnp.where(row == tile - 1, rcv[sub, 1, lat, m : m + 1, l], pltpu.roll(x, tile - 1, 0))
                        south = lambda: f[m, lat, :, l]
                        north = lambda: f[m, lat + 2, :, l]
                        v = vc * x + va * pick(zspan[c], west, east) + vb * pick(mspan[c], south, north)
                        acc[m] = v * v if c == 0 else acc[m] + v * v
                        q = pl.ds(pl.multiple_of((i * count + m) * tile, 16), tile)
                        gbuf[q, l] = v
                        hi = v.astype(jnp.bfloat16)
                        lhs[q, l] = hi
                        lhs[q, width + c * LANES : width + (c + 1) * LANES] = (v - hi.astype(jnp.float32)).astype(jnp.bfloat16)
                for m in range(count):
                    q = pl.ds(pl.multiple_of((i * count + m) * tile, 16), tile)
                    e = jnp.sum(acc[m], axis=1, keepdims=True) * (0.05 / bins)
                    ebuf[q, :] = jnp.broadcast_to(e, (tile, LANES))

            chunk = 2 * LANES
            for c in range(0, width, chunk):
                l = slice(c, c + chunk)
                left_side = jnp.concatenate([lhs[...], lhs[:, :width]], axis=1)
                t = jnp.dot(left_side, rk[:, l], preferred_element_type=jnp.float32)
                for i in range(block):
                    lat = g * block + i
                    w = tw[pl.ds(pl.multiple_of(lat * tile, 8), tile), l]
                    for m in range(count):
                        k = (i * count + m) * tile
                        e = ebuf[k : k + tile, :]
                        e = jnp.concatenate([e] * (chunk // LANES), axis=1)
                        write(m, lat, l, gbuf[k : k + tile, l] * (w - e) + t[k : k + tile])
            if sub == 0:
                for i in range(block):
                    keep_edges(1, f1, g * block + i)
                for c in halo_copies(1, g):
                    c.start()
            else:
                out_copy(g).start()

    def out_copy(g):
        r = pl.ds(pl.multiple_of(g * block * tile, 8), block * tile)
        return pltpu.make_async_copy(mv.at[:, r], out_hbm.at[:, r], out_sem.at[g])

    def to_f1(m, lat, l, v):
        f1[m, lat + 1, :, l] = v

    def to_out(m, lat, l, v):
        stop = min(l.stop, bins)
        mv[m, pl.ds(pl.multiple_of(lat * tile, 8), tile), l.start : stop] = v[:, : stop - l.start]

    substep(0, f0, to_f1)
    substep(1, f1, to_out)

    for o in range(1, n):
        rs_copy(o).wait_send()
        ag_copy(o).wait_send()

    @pl.loop(0, blocks)
    def _(g):
        for sub in range(2):
            for c in halo_copies(sub, g):
                c.wait_send()
        out_copy(g).wait()


def shards(members, control, sea_mask, depth_class, wind_dir, growth, rate_kernel):
    count, tile, rows_lat, bins = members.shape
    n, lons = lax.axis_size("mem"), lax.axis_size("lon")
    cells = rows_lat * tile
    width = round_up(bins, 2 * LANES)
    part = cells // n
    block = 3 if rows_lat % 3 == 0 else 1
    blocks = rows_lat // block
    tab, wind, one, cs, sn = constants(bins, width)

    m = members.transpose(0, 2, 1, 3).reshape(count, cells, bins)
    c = control.transpose(1, 0, 2).reshape(cells, control.shape[2])
    flat = lambda x: x.T.reshape(cells, 1)
    sea, depth, wdir = flat(sea_mask), flat(depth_class), flat(wind_dir)
    slot = jnp.arange(LANES)[None, :]
    hot = (slot == depth) | (slot == wdir + CLASSES) | (slot == CLASSES + DIRS)
    hot = jnp.where(hot & (sea != 0), 1.0, 0.0).astype(jnp.float32)
    spread = jnp.pad(jnp.tile(growth, DIRS), (0, width - bins))[None]

    f32, bf16 = jnp.float32, jnp.bfloat16
    vmem = pl.BlockSpec(memory_space=pltpu.VMEM)
    hbm = pl.BlockSpec(memory_space=pl.ANY)
    field = pltpu.VMEM((count, rows_lat + 2, tile, width), f32)
    table = pltpu.VMEM((cells, width), f32)
    rows = block * count * tile
    out = pl.pallas_call(
        functools.partial(
            kernel, n, lons, count, rows_lat, tile, bins, width, spans(cs), spans(sn), count * n,
        ),
        out_shape=jax.ShapeDtypeStruct((count, cells, bins), f32),
        in_specs=[hbm, hbm, hbm] + [vmem] * 5,
        out_specs=hbm,
        scratch_shapes=[
            pltpu.VMEM((count, cells, bins), f32),
            pltpu.VMEM((cells, control.shape[2]), f32),
            pltpu.VMEM((bins, bins), f32),
            pltpu.VMEM((cells, bins), f32),
            pltpu.VMEM((cells, bins), f32),
            pltpu.VMEM((n - 1, part, bins), f32),
            pltpu.VMEM((cells, bins), f32),
            field, field, table, table, table, table,
            pltpu.VMEM((3 * width, width), bf16),
            pltpu.VMEM((rows, 2 * width), bf16),
            pltpu.VMEM((rows, width), f32),
            pltpu.VMEM((rows, LANES), f32),
            pltpu.VMEM((2, 2, rows_lat, count, width), f32),
            pltpu.VMEM((2, 2, rows_lat, count, width), f32),
            pltpu.SemaphoreType.DMA((n,)),
            pltpu.SemaphoreType.DMA((2,)),
            pltpu.SemaphoreType.DMA((blocks,)),
            pltpu.SemaphoreType.DMA((n - 1,)),
            pltpu.SemaphoreType.DMA((n - 1,)),
            pltpu.SemaphoreType.DMA((n - 1,)),
            pltpu.SemaphoreType.DMA((n - 1,)),
            pltpu.SemaphoreType.DMA((2, 2, blocks)),
            pltpu.SemaphoreType.DMA((2, 2, blocks)),
        ],
        compiler_params=pltpu.CompilerParams(
            collective_id=0, has_side_effects=True, vmem_limit_bytes=58 * 1024 * 1024
        ),
    )(m, c, rate_kernel, hot, jnp.asarray(tab), jnp.asarray(wind), jnp.asarray(one), spread)
    return out.reshape(count, rows_lat, tile, bins).transpose(0, 2, 1, 3)


def solution(mesh):
    return jax.shard_map(
        shards,
        mesh=mesh,
        in_specs=(
            P("mem", "lon", None, None),
            P("lon", None, "mem"),
            P("lon", None),
            P("lon", None),
            P("lon", None),
            P(),
            P(),
        ),
        out_specs=P("mem", "lon", None, None),
        check_vma=False,
    )
```

```python
import functools
import math

import jax
import jax.numpy as jnp
import numpy as np
from jax import lax
from jax.experimental import pallas as pl
from jax.experimental.pallas import tpu as pltpu
from jax.sharding import PartitionSpec as P

DIRS = 24
FREQS = 30
LANES = 128
CLASSES = 4
SLOTS = 32


def round_up(x, to):
    return -(-x // to) * to


def constants(bins, width):
    frequency = 0.04 * 1.1 ** np.arange(FREQS, dtype=np.float64)
    deep = 9.81 / (4.0 * math.pi * frequency)
    shallow = np.sqrt(9.81 * np.array([10.0, 30.0, 80.0, 200.0]))
    speed = 0.7 * np.minimum(deep[None], shallow[:, None]) / (9.81 / (4.0 * math.pi * 0.04))
    angles = 2.0 * math.pi * np.arange(DIRS) / DIRS
    cos, sin = np.cos(angles), np.sin(angles)
    cos[np.abs(cos) < 1e-9] = 0.0
    sin[np.abs(sin) < 1e-9] = 0.0
    lift = lambda v: (v[None, :, None] * speed[:, None, :]).reshape(CLASSES, bins)
    a, b = lift(np.abs(cos)), lift(np.abs(sin))
    tab = np.zeros((SLOTS, 3 * width), np.float32)
    tab[:CLASSES, :bins] = a
    tab[:CLASSES, width : width + bins] = b
    tab[:CLASSES, 2 * width : 2 * width + bins] = -(a + b)
    tab[CLASSES + DIRS, 2 * width : 2 * width + bins] = 1.0
    rel = np.arange(DIRS)[None, :] - np.arange(DIRS)[:, None]
    align = np.maximum(np.cos(2.0 * math.pi * rel / DIRS), 0.0)
    wind = np.zeros((SLOTS + FREQS + 2, width), np.float32)
    wind[CLASSES : CLASSES + DIRS, :bins] = 0.1 * np.repeat(align, FREQS, axis=1)
    wind[SLOTS : SLOTS + FREQS, :bins] = np.tile(np.eye(FREQS), (1, DIRS))
    cs = np.zeros(width, np.int32)
    sn = np.zeros(width, np.int32)
    cs[:bins] = np.repeat(np.sign(cos), FREQS)
    sn[:bins] = np.repeat(np.sign(sin), FREQS)
    return tab, wind, cs, sn


def spans(sign):
    out = []
    for c in range(len(sign) // LANES):
        s = sign[c * LANES : (c + 1) * LANES]
        if (s >= 0).all():
            out.append(1)
        elif (s <= 0).all():
            out.append(-1)
        else:
            pos = np.nonzero(s > 0)[0]
            out.append((int(pos[0]), int(pos[-1]) + 1))
            assert (s[pos[0] : pos[-1] + 1] >= 0).all()
    return out


def kernel(
    n, lons, count, rows_lat, tile, bins, width, zspan, mspan, total_members,
    m_hbm, ctrl_hbm, k_hbm, sea_ref, depth_ref, wdir_ref, tab_ref, wind_ref, growth_ref,
    out_hbm,
    mv, ctrlv, kv, ctrlp, dl, rsb, dfull, oh_ref, f0, f1, ta, tb, tc, tw, rk, lhs, gbuf, ebuf,
    snd, rcv,
    m_sem, in_sem, out_sem, rs_s, rs_r, ag_s, ag_r, h_s, h_r,
):
    me = lax.axis_index("mem")
    at = lax.axis_index("lon")
    right = lax.rem(at + 1, lons)
    left = lax.rem(at + lons - 1, lons)
    cells = rows_lat * tile
    quarter = cells // 4
    bits = n.bit_length() - 1
    ways = (tuple(range(bits)), tuple(reversed(range(bits))))
    cols = width // LANES
    block = 3 if rows_lat % 3 == 0 else 1
    blocks = rows_lat // block
    own_bins = ctrlv.shape[1]

    def bit(b):
        return lax.rem(me // (1 << b), 2)

    def partner(b):
        return me + (1 - 2 * bit(b)) * (1 << b)

    def rows(start, size):
        return pl.ds(pl.multiple_of(start, 8), size)

    def kept(h, s):
        start, size = h * 2 * quarter, 2 * quarter
        for b in ways[h][:s]:
            size //= 2
            start = start + bit(b) * size
        return start, size

    def given(h, s):
        start, size = kept(h, s)
        size //= 2
        return start + (1 - bit(ways[h][s])) * size, size

    quarters = [given(0, 0)[0], given(1, 0)[0], kept(0, 1)[0], kept(1, 1)[0]]

    def m_copy(q):
        r = rows(quarters[q], quarter)
        return pltpu.make_async_copy(m_hbm.at[:, r], mv.at[:, r], m_sem.at[q])

    c_copy = pltpu.make_async_copy(ctrl_hbm, ctrlv, in_sem.at[0])
    k_copy = pltpu.make_async_copy(k_hbm, kv, in_sem.at[1])
    c_copy.start()
    for q in range(4):
        m_copy(q).start()
    k_copy.start()

    barrier = pltpu.get_barrier_semaphore()
    for b in range(bits):
        pl.semaphore_signal(barrier, inc=1, device_id={"mem": partner(b)}, device_id_type=pl.DeviceIdType.MESH)
    for side in (left, right):
        pl.semaphore_signal(barrier, inc=1, device_id={"lon": side}, device_id_type=pl.DeviceIdType.MESH)

    ctrlp[...] = jnp.zeros_like(ctrlp)
    c_copy.wait()
    for k in range(n):
        @pl.when(me == k)
        def _():
            ctrlp[:, k * own_bins : (k + 1) * own_bins] = ctrlv[...]

    pl.semaphore_wait(barrier, bits + 2)

    def rs_copy(h, s):
        start, size = given(h, s)
        return pltpu.make_async_remote_copy(
            src_ref=dl.at[rows(start, size)], dst_ref=rsb.at[h, pl.ds(2 * quarter - 2 * size, size)],
            send_sem=rs_s.at[h, s], recv_sem=rs_r.at[h, s],
            device_id={"mem": partner(ways[h][s])}, device_id_type=pl.DeviceIdType.MESH,
        )

    def ag_copy(h, s):
        r = rows(*kept(h, s + 1))
        return pltpu.make_async_remote_copy(
            src_ref=dfull.at[r], dst_ref=dfull.at[r], send_sem=ag_s.at[h, s], recv_sem=ag_r.at[h, s],
            device_id={"mem": partner(ways[h][s])}, device_id_type=pl.DeviceIdType.MESH,
        )

    def ag_arrival(h, s):
        r = rows(*given(h, s))
        return pltpu.make_async_remote_copy(
            src_ref=dfull.at[r], dst_ref=dfull.at[r], send_sem=ag_s.at[h, s], recv_sem=ag_r.at[h, s],
            device_id={"mem": partner(ways[h][s])}, device_id_type=pl.DeviceIdType.MESH,
        )

    def local_sum(q):
        m_copy(q).wait()

        @pl.loop(0, quarter // 16)
        def _(i):
            r = rows(quarters[q] + i * 16, 16)
            s = mv[0, r, :]
            for m in range(1, count):
                s = s + mv[m, r, :]
            dl[r, :] = ctrlp[r, :] - s * (1.0 / total_members)

    def take(h, s):
        rs_copy(h, s).wait_recv()
        start, size = kept(h, s + 1)
        to = dl if s < bits - 1 else dfull
        at_row = 2 * quarter - 2 * size

        @pl.loop(0, size // 8)
        def _(i):
            r = rows(start + i * 8, 8)
            to[r, :] = dl[r, :] + rsb[h, rows(at_row + i * 8, 8), :]

    for q in (0, 1):
        local_sum(q)
        rs_copy(q, 0).start()
    for q in (2, 3):
        local_sum(q)

    slot = lax.broadcasted_iota(jnp.int32, (SLOTS, tile), 0)
    for i in range(rows_lat):
        hot = (slot == depth_ref[i : i + 1, :]) | (slot == wdir_ref[i : i + 1, :] + CLASSES) | (slot == CLASSES + DIRS)
        hot = jnp.where(hot & (sea_ref[i : i + 1, :] != 0), 1.0, 0.0)
        oh_ref[i * tile : (i + 1) * tile, :] = hot.T

    def split(x):
        hi = x.astype(jnp.bfloat16)
        x = x - hi.astype(jnp.float32)
        mid = x.astype(jnp.bfloat16)
        return jnp.concatenate([hi, mid, (x - mid.astype(jnp.float32)).astype(jnp.bfloat16)], axis=0)

    spread = jnp.dot(
        jnp.broadcast_to(growth_ref[...], (8, SLOTS)), wind_ref[SLOTS:, :],
        precision=lax.Precision.HIGHEST, preferred_element_type=jnp.float32,
    )
    slots = lax.broadcasted_iota(jnp.int32, (SLOTS, width), 0)
    lanes = lax.broadcasted_iota(jnp.int32, (SLOTS, width), 1)
    gains = wind_ref[:SLOTS, :] * spread[0:1, :]
    gains = jnp.where((slots == CLASSES + DIRS) & (lanes < bins), 1.0, gains)
    oh = oh_ref[...].astype(jnp.bfloat16)
    oh = jnp.concatenate([oh, oh, oh], axis=1)
    for to, tab in (
        (ta, tab_ref[:, :width]), (tb, tab_ref[:, width : 2 * width]), (tc, tab_ref[:, 2 * width :]), (tw, gains),
    ):
        to[...] = jnp.dot(oh, split(tab), preferred_element_type=jnp.float32)

    def prepare():
        rk[...] = jnp.zeros_like(rk)
        k_copy.wait()

        @pl.loop(0, bins // 16)
        def _(i):
            k = kv[pl.ds(pl.multiple_of(i * 16, 16), 16), :] * 0.1
            hi = k.astype(jnp.bfloat16)
            lo = (k - hi.astype(jnp.float32)).astype(jnp.bfloat16)
            rk[pl.ds(pl.multiple_of(i * 16, 16), 16), :bins] = hi
            rk[pl.ds(pl.multiple_of(width + i * 16, 16), 16), :bins] = hi
            rk[pl.ds(pl.multiple_of(2 * width + i * 16, 16), 16), :bins] = lo

        zero = jnp.zeros((tile, width), jnp.float32)
        for m in range(count):
            for f in (f0, f1):
                f[m, 0] = zero
                f[m, rows_lat + 1] = zero

            @pl.loop(0, rows_lat)
            def _(i):
                f0[m, i + 1, :, width - LANES :] = jnp.zeros((tile, LANES), jnp.float32)

    def halo_copies(sub, g):
        r = pl.ds(g * block, block)
        made = []
        for side, to in ((0, right), (1, left)):
            made.append(pltpu.make_async_remote_copy(
                src_ref=snd.at[sub, side, r], dst_ref=rcv.at[sub, side, r],
                send_sem=h_s.at[sub, side, g], recv_sem=h_r.at[sub, side, g],
                device_id={"lon": to}, device_id_type=pl.DeviceIdType.MESH,
            ))
        return made

    def keep_edges(sub, f, lat):
        snd[sub, 0, lat] = jnp.concatenate([f[m, lat + 1, tile - 1 : tile, :] for m in range(count)], axis=0)
        snd[sub, 1, lat] = jnp.concatenate([f[m, lat + 1, 0:1, :] for m in range(count)], axis=0)

    for s in range(1, bits):
        for h in (0, 1):
            take(h, s - 1)
            rs_copy(h, s).start()
    def recentre(g):
        @pl.loop(0, block)
        def _(i):
            lat = g * block + i
            r = pl.ds(pl.multiple_of(lat * tile, 8), tile)
            sea = oh_ref[r, CLASSES + DIRS : CLASSES + DIRS + 1] > 0.5
            d = dfull[r, :]
            for m in range(count):
                f0[m, lat + 1, :, :bins] = jnp.where(sea, mv[m, r, :] + d, 0.0)
            keep_edges(0, f0, lat)
        for c in halo_copies(0, g):
            c.start()

    prepare()
    for h in (0, 1):
        take(h, bits - 1)
        ag_copy(h, bits - 1).start()
    for s in reversed(range(bits - 1)):
        for h in (0, 1):
            ag_arrival(h, s + 1).wait_recv()
            ag_copy(h, s).start()
    for h in (0, 1):
        recentre(2 * h + bit(ways[h][0]))
    for h in (0, 1):
        ag_arrival(h, 0).wait_recv()
        recentre(2 * h + 1 - bit(ways[h][0]))

    row = lax.broadcasted_iota(jnp.int32, (tile, LANES), 0)
    lane = lax.broadcasted_iota(jnp.int32, (tile, LANES), 1)

    def pick(span, behind, ahead):
        if span == 1:
            return behind()
        if span == -1:
            return ahead()
        return jnp.where((lane >= span[0]) & (lane < span[1]), behind(), ahead())

    def substep(sub, f, write):
        @pl.loop(0, blocks)
        def _(g):
            for c in halo_copies(sub, g):
                c.wait_recv()

            @pl.loop(0, block)
            def _(i):
                lat = g * block + i
                r = pl.ds(pl.multiple_of(lat * tile, 8), tile)
                acc = [None] * count
                for c in range(cols):
                    l = slice(c * LANES, (c + 1) * LANES)
                    va, vb, vc = ta[r, l], tb[r, l], tc[r, l]
                    for m in range(count):
                        x = f[m, lat + 1, :, l]
                        west = lambda: jnp.where(row == 0, rcv[sub, 0, lat, m : m + 1, l], pltpu.roll(x, 1, 0))
                        east = lambda: jnp.where(row == tile - 1, rcv[sub, 1, lat, m : m + 1, l], pltpu.roll(x, tile - 1, 0))
                        south = lambda: f[m, lat, :, l]
                        north = lambda: f[m, lat + 2, :, l]
                        v = vc * x + va * pick(zspan[c], west, east) + vb * pick(mspan[c], south, north)
                        acc[m] = v * v if c == 0 else acc[m] + v * v
                        q = pl.ds(pl.multiple_of((i * count + m) * tile, 16), tile)
                        gbuf[q, l] = v
                        hi = v.astype(jnp.bfloat16)
                        lhs[q, l] = hi
                        lhs[q, width + c * LANES : width + (c + 1) * LANES] = (v - hi.astype(jnp.float32)).astype(jnp.bfloat16)
                for m in range(count):
                    q = pl.ds(pl.multiple_of((i * count + m) * tile, 16), tile)
                    e = jnp.sum(acc[m], axis=1, keepdims=True) * (0.05 / bins)
                    ebuf[q, :] = jnp.broadcast_to(e, (tile, LANES))

            chunk = 2 * LANES
            for c in range(0, width, chunk):
                l = slice(c, c + chunk)
                left_side = jnp.concatenate([lhs[...], lhs[:, :width]], axis=1)
                t = jnp.dot(left_side, rk[:, l], preferred_element_type=jnp.float32)
                for i in range(block):
                    lat = g * block + i
                    w = tw[pl.ds(pl.multiple_of(lat * tile, 8), tile), l]
                    for m in range(count):
                        k = (i * count + m) * tile
                        e = ebuf[k : k + tile, :]
                        e = jnp.concatenate([e] * (chunk // LANES), axis=1)
                        write(m, lat, l, gbuf[k : k + tile, l] * (w - e) + t[k : k + tile])
            if sub == 0:
                for i in range(block):
                    keep_edges(1, f1, g * block + i)
                for c in halo_copies(1, g):
                    c.start()
            else:
                out_copy(g).start()

    def out_copy(g):
        r = pl.ds(pl.multiple_of(g * block * tile, 8), block * tile)
        return pltpu.make_async_copy(mv.at[:, r], out_hbm.at[:, r], out_sem.at[g])

    def to_f1(m, lat, l, v):
        f1[m, lat + 1, :, l] = v

    def to_out(m, lat, l, v):
        stop = min(l.stop, bins)
        mv[m, pl.ds(pl.multiple_of(lat * tile, 8), tile), l.start : stop] = v[:, : stop - l.start]

    substep(0, f0, to_f1)
    substep(1, f1, to_out)

    for h in (0, 1):
        for s in range(bits):
            rs_copy(h, s).wait_send()
            ag_copy(h, s).wait_send()

    @pl.loop(0, blocks)
    def _(g):
        for sub in range(2):
            for c in halo_copies(sub, g):
                c.wait_send()
        out_copy(g).wait()


def shards(members, control, sea_mask, depth_class, wind_dir, growth, rate_kernel):
    count, tile, rows_lat, bins = members.shape
    n, lons = lax.axis_size("mem"), lax.axis_size("lon")
    cells = rows_lat * tile
    width = round_up(bins, 2 * LANES)
    bits = n.bit_length() - 1
    assert n == 1 << bits and cells % (4 * n) == 0
    block = 3 if rows_lat % 3 == 0 else 1
    blocks = rows_lat // block
    tab, wind, cs, sn = constants(bins, width)

    m = members.transpose(0, 2, 1, 3).reshape(count, cells, bins)
    c = control.transpose(1, 0, 2).reshape(cells, control.shape[2])
    spread = jnp.pad(growth, (0, SLOTS - FREQS))[None]

    f32, bf16 = jnp.float32, jnp.bfloat16
    vmem = pl.BlockSpec(memory_space=pltpu.VMEM)
    hbm = pl.BlockSpec(memory_space=pl.ANY)
    field = pltpu.VMEM((count, rows_lat + 2, tile, width), f32)
    table = pltpu.VMEM((cells, width), f32)
    rows = block * count * tile
    out = pl.pallas_call(
        functools.partial(
            kernel, n, lons, count, rows_lat, tile, bins, width, spans(cs), spans(sn), count * n,
        ),
        out_shape=jax.ShapeDtypeStruct((count, cells, bins), f32),
        in_specs=[hbm, hbm, hbm] + [vmem] * 6,
        out_specs=hbm,
        scratch_shapes=[
            pltpu.VMEM((count, cells, bins), f32),
            pltpu.VMEM((cells, control.shape[2]), f32),
            pltpu.VMEM((bins, bins), f32),
            pltpu.VMEM((cells, bins), f32),
            pltpu.VMEM((cells, bins), f32),
            pltpu.VMEM((2, cells // 2, bins), f32),
            pltpu.VMEM((cells, bins), f32),
            pltpu.VMEM((cells, SLOTS), f32),
            field, field, table, table, table, table,
            pltpu.VMEM((3 * width, width), bf16),
            pltpu.VMEM((rows, 2 * width), bf16),
            pltpu.VMEM((rows, width), f32),
            pltpu.VMEM((rows, LANES), f32),
            pltpu.VMEM((2, 2, rows_lat, count, width), f32),
            pltpu.VMEM((2, 2, rows_lat, count, width), f32),
            pltpu.SemaphoreType.DMA((4,)),
            pltpu.SemaphoreType.DMA((2,)),
            pltpu.SemaphoreType.DMA((blocks,)),
            pltpu.SemaphoreType.DMA((2, bits)),
            pltpu.SemaphoreType.DMA((2, bits)),
            pltpu.SemaphoreType.DMA((2, bits)),
            pltpu.SemaphoreType.DMA((2, bits)),
            pltpu.SemaphoreType.DMA((2, 2, blocks)),
            pltpu.SemaphoreType.DMA((2, 2, blocks)),
        ],
        compiler_params=pltpu.CompilerParams(
            collective_id=0, has_side_effects=True, vmem_limit_bytes=58 * 1024 * 1024
        ),
    )(m, c, rate_kernel, sea_mask.T, depth_class.T, wind_dir.T, jnp.asarray(tab), jnp.asarray(wind), spread)
    return out.reshape(count, rows_lat, tile, bins).transpose(0, 2, 1, 3)


def solution(mesh):
    return jax.shard_map(
        shards,
        mesh=mesh,
        in_specs=(
            P("mem", "lon", None, None),
            P("lon", None, "mem"),
            P("lon", None),
            P("lon", None),
            P("lon", None),
            P(),
            P(),
        ),
        out_specs=P("mem", "lon", None, None),
        check_vma=False,
    )
```

```python
import functools
import math

import jax
import jax.numpy as jnp
import numpy as np
from jax import lax
from jax.experimental import pallas as pl
from jax.experimental.pallas import tpu as pltpu
from jax.sharding import PartitionSpec as P

DIRS = 24
FREQS = 30
LANES = 128
CLASSES = 4
SLOTS = 32


def round_up(x, to):
    return -(-x // to) * to


def constants(bins, width):
    frequency = 0.04 * 1.1 ** np.arange(FREQS, dtype=np.float64)
    deep = 9.81 / (4.0 * math.pi * frequency)
    shallow = np.sqrt(9.81 * np.array([10.0, 30.0, 80.0, 200.0]))
    speed = 0.7 * np.minimum(deep[None], shallow[:, None]) / (9.81 / (4.0 * math.pi * 0.04))
    angles = 2.0 * math.pi * np.arange(DIRS) / DIRS
    cos, sin = np.cos(angles), np.sin(angles)
    cos[np.abs(cos) < 1e-9] = 0.0
    sin[np.abs(sin) < 1e-9] = 0.0
    lift = lambda v: (v[None, :, None] * speed[:, None, :]).reshape(CLASSES, bins)
    a, b = lift(np.abs(cos)), lift(np.abs(sin))
    tab = np.zeros((SLOTS, 3 * width), np.float32)
    tab[:CLASSES, :bins] = a
    tab[:CLASSES, width : width + bins] = b
    tab[:CLASSES, 2 * width : 2 * width + bins] = -(a + b)
    tab[CLASSES + DIRS, 2 * width : 2 * width + bins] = 1.0
    rel = np.arange(DIRS)[None, :] - np.arange(DIRS)[:, None]
    align = np.maximum(np.cos(2.0 * math.pi * rel / DIRS), 0.0)
    wind = np.zeros((SLOTS + FREQS + 2, width), np.float32)
    wind[CLASSES : CLASSES + DIRS, :bins] = 0.1 * np.repeat(align, FREQS, axis=1)
    wind[SLOTS : SLOTS + FREQS, :bins] = np.tile(np.eye(FREQS), (1, DIRS))
    cs = np.zeros(width, np.int32)
    sn = np.zeros(width, np.int32)
    cs[:bins] = np.repeat(np.sign(cos), FREQS)
    sn[:bins] = np.repeat(np.sign(sin), FREQS)
    return tab, wind, cs, sn


def spans(sign):
    out = []
    for c in range(len(sign) // LANES):
        s = sign[c * LANES : (c + 1) * LANES]
        if (s >= 0).all():
            out.append(1)
        elif (s <= 0).all():
            out.append(-1)
        else:
            pos = np.nonzero(s > 0)[0]
            out.append((int(pos[0]), int(pos[-1]) + 1))
            assert (s[pos[0] : pos[-1] + 1] >= 0).all()
    return out


def kernel(
    n, lons, count, rows_lat, tile, bins, width, zspan, mspan, total_members,
    m_hbm, ctrl_hbm, k_hbm, sea_ref, depth_ref, wdir_ref, tab_ref, wind_ref, growth_ref,
    out_hbm,
    mv, ctrlv, kv, ctrlp, dl, rsb, dfull, oh_ref, f0, f1, ta, tb, tc, tw, rk, lhs, gbuf, ebuf, fd, gm, td,
    snd, rcv,
    m_sem, in_sem, out_sem, rs_s, rs_r, ag_s, ag_r, h_s, h_r,
):
    me = lax.axis_index("mem")
    at = lax.axis_index("lon")
    right = lax.rem(at + 1, lons)
    left = lax.rem(at + lons - 1, lons)
    cells = rows_lat * tile
    quarter = cells // 4
    bits = n.bit_length() - 1
    ways = (tuple(range(bits)), tuple(reversed(range(bits))))
    cols = width // LANES
    block = 3 if rows_lat % 3 == 0 else 1
    blocks = rows_lat // block
    own_bins = ctrlv.shape[1]

    def bit(b):
        return lax.rem(me // (1 << b), 2)

    def partner(b):
        return me + (1 - 2 * bit(b)) * (1 << b)

    def rows(start, size):
        return pl.ds(pl.multiple_of(start, 8), size)

    def kept(h, s):
        start, size = h * 2 * quarter, 2 * quarter
        for b in ways[h][:s]:
            size //= 2
            start = start + bit(b) * size
        return start, size

    def given(h, s):
        start, size = kept(h, s)
        size //= 2
        return start + (1 - bit(ways[h][s])) * size, size

    quarters = [given(0, 0)[0], given(1, 0)[0], kept(0, 1)[0], kept(1, 1)[0]]

    def m_copy(q):
        r = rows(quarters[q], quarter)
        return pltpu.make_async_copy(m_hbm.at[:, r], mv.at[:, r], m_sem.at[q])

    c_copy = pltpu.make_async_copy(ctrl_hbm, ctrlv, in_sem.at[0])
    k_copy = pltpu.make_async_copy(k_hbm, kv, in_sem.at[1])
    c_copy.start()
    for q in range(4):
        m_copy(q).start()
    k_copy.start()

    barrier = pltpu.get_barrier_semaphore()
    for b in range(bits):
        pl.semaphore_signal(barrier, inc=1, device_id={"mem": partner(b)}, device_id_type=pl.DeviceIdType.MESH)
    for side in (left, right):
        pl.semaphore_signal(barrier, inc=1, device_id={"lon": side}, device_id_type=pl.DeviceIdType.MESH)

    ctrlp[...] = jnp.zeros_like(ctrlp)
    c_copy.wait()
    for k in range(n):
        @pl.when(me == k)
        def _():
            ctrlp[:, k * own_bins : (k + 1) * own_bins] = ctrlv[...]

    pl.semaphore_wait(barrier, bits + 2)

    def rs_copy(h, s):
        start, size = given(h, s)
        return pltpu.make_async_remote_copy(
            src_ref=dl.at[rows(start, size)], dst_ref=rsb.at[h, pl.ds(2 * quarter - 2 * size, size)],
            send_sem=rs_s.at[h, s], recv_sem=rs_r.at[h, s],
            device_id={"mem": partner(ways[h][s])}, device_id_type=pl.DeviceIdType.MESH,
        )

    def ag_copy(h, s):
        r = rows(*kept(h, s + 1))
        return pltpu.make_async_remote_copy(
            src_ref=dfull.at[r], dst_ref=dfull.at[r], send_sem=ag_s.at[h, s], recv_sem=ag_r.at[h, s],
            device_id={"mem": partner(ways[h][s])}, device_id_type=pl.DeviceIdType.MESH,
        )

    def ag_arrival(h, s):
        r = rows(*given(h, s))
        return pltpu.make_async_remote_copy(
            src_ref=dfull.at[r], dst_ref=dfull.at[r], send_sem=ag_s.at[h, s], recv_sem=ag_r.at[h, s],
            device_id={"mem": partner(ways[h][s])}, device_id_type=pl.DeviceIdType.MESH,
        )

    def local_sum(q):
        m_copy(q).wait()

        @pl.loop(0, quarter // 16)
        def _(i):
            r = rows(quarters[q] + i * 16, 16)
            s = mv[0, r, :]
            for m in range(1, count):
                s = s + mv[m, r, :]
            dl[r, :] = ctrlp[r, :] - s * (1.0 / total_members)

    def take(h, s):
        rs_copy(h, s).wait_recv()
        start, size = kept(h, s + 1)
        to = dl if s < bits - 1 else dfull
        at_row = 2 * quarter - 2 * size

        @pl.loop(0, size // 8)
        def _(i):
            r = rows(start + i * 8, 8)
            to[r, :] = dl[r, :] + rsb[h, rows(at_row + i * 8, 8), :]

    for q in (0, 1):
        local_sum(q)
        rs_copy(q, 0).start()
    for q in (2, 3):
        local_sum(q)

    slot = lax.broadcasted_iota(jnp.int32, (SLOTS, tile), 0)
    for i in range(rows_lat):
        hot = (slot == depth_ref[i : i + 1, :]) | (slot == wdir_ref[i : i + 1, :] + CLASSES) | (slot == CLASSES + DIRS)
        hot = jnp.where(hot & (sea_ref[i : i + 1, :] != 0), 1.0, 0.0)
        oh_ref[i * tile : (i + 1) * tile, :] = hot.T

    def split(x):
        hi = x.astype(jnp.bfloat16)
        x = x - hi.astype(jnp.float32)
        mid = x.astype(jnp.bfloat16)
        return jnp.concatenate([hi, mid, (x - mid.astype(jnp.float32)).astype(jnp.bfloat16)], axis=0)

    rates = jnp.concatenate([growth_ref[...], jnp.zeros((1, SLOTS - FREQS), jnp.float32)], axis=1)
    spread = jnp.dot(
        jnp.broadcast_to(rates, (8, SLOTS)), wind_ref[SLOTS:, :],
        precision=lax.Precision.HIGHEST, preferred_element_type=jnp.float32,
    )
    slots = lax.broadcasted_iota(jnp.int32, (SLOTS, width), 0)
    lanes = lax.broadcasted_iota(jnp.int32, (SLOTS, width), 1)
    gains = wind_ref[:SLOTS, :] * spread[0:1, :]
    gains = jnp.where((slots == CLASSES + DIRS) & (lanes < bins), 1.0, gains)
    oh = oh_ref[...].astype(jnp.bfloat16)
    oh = jnp.concatenate([oh, oh, oh], axis=1)
    for to, tab in (
        (ta, tab_ref[:, :width]), (tb, tab_ref[:, width : 2 * width]), (tc, tab_ref[:, 2 * width :]), (tw, gains),
    ):
        to[...] = jnp.dot(oh, split(tab), preferred_element_type=jnp.float32)

    def prepare():
        rk[...] = jnp.zeros_like(rk)
        k_copy.wait()

        @pl.loop(0, bins // 16)
        def _(i):
            k = kv[pl.ds(pl.multiple_of(i * 16, 16), 16), :] * 0.1
            hi = k.astype(jnp.bfloat16)
            lo = (k - hi.astype(jnp.float32)).astype(jnp.bfloat16)
            rk[pl.ds(pl.multiple_of(i * 16, 16), 16), :bins] = hi
            rk[pl.ds(pl.multiple_of(width + i * 16, 16), 16), :bins] = hi
            rk[pl.ds(pl.multiple_of(2 * width + i * 16, 16), 16), :bins] = lo

    def halo_copies(sub, g):
        r = pl.ds(g * block, block)
        made = []
        for side, to in ((0, right), (1, left)):
            made.append(pltpu.make_async_remote_copy(
                src_ref=snd.at[sub, side, r], dst_ref=rcv.at[sub, side, r],
                send_sem=h_s.at[sub, side, g], recv_sem=h_r.at[sub, side, g],
                device_id={"lon": to}, device_id_type=pl.DeviceIdType.MESH,
            ))
        return made

    def keep_edges(sub, f, lat):
        picks = range(count) if sub < 2 else [0] * count
        snd[sub, 0, lat] = jnp.concatenate([f[m, lat + 1, tile - 1 : tile, :] for m in picks], axis=0)
        snd[sub, 1, lat] = jnp.concatenate([f[m, lat + 1, 0:1, :] for m in picks], axis=0)

    zero = jnp.zeros((tile, width), jnp.float32)
    for m in range(count):
        for f in (f0, f1):
            f[m, 0] = zero
            f[m, rows_lat + 1] = zero

        @pl.loop(0, rows_lat)
        def _(i):
            f0[m, i + 1, :, width - LANES :] = jnp.zeros((tile, LANES), jnp.float32)
    fd[...] = jnp.zeros_like(fd)

    def recentre(sub, g):
        @pl.loop(0, block, unroll=True)
        def _(i):
            lat = g * block + i
            r = pl.ds(pl.multiple_of(lat * tile, 8), tile)
            sea = oh_ref[r, CLASSES + DIRS : CLASSES + DIRS + 1] > 0.5
            if sub == 0:
                for m in range(count):
                    f0[m, lat + 1, :, :bins] = jnp.where(sea, mv[m, r, :], 0.0)
                keep_edges(0, f0, lat)
            else:
                fd[0, lat + 1, :, :bins] = jnp.where(sea, dfull[r, :], 0.0)
                keep_edges(2, fd, lat)
        for c in halo_copies(sub, g):
            c.start()

    row = lax.broadcasted_iota(jnp.int32, (tile, LANES), 0)
    lane = lax.broadcasted_iota(jnp.int32, (tile, LANES), 1)

    def pick(span, behind, ahead):
        if span == 1:
            return behind()
        if span == -1:
            return ahead()
        return jnp.where((lane >= span[0]) & (lane < span[1]), behind(), ahead())

    def advect(sub, f, lat, many, keep):
        r = pl.ds(pl.multiple_of(lat * tile, 8), tile)
        for c in range(cols):
            l = slice(c * LANES, (c + 1) * LANES)
            va, vb, vc = ta[r, l], tb[r, l], tc[r, l]
            for m in range(many):
                x = f[m, lat + 1, :, l]
                west = lambda: jnp.where(row == 0, rcv[sub, 0, lat, m : m + 1, l], pltpu.roll(x, 1, 0))
                east = lambda: jnp.where(row == tile - 1, rcv[sub, 1, lat, m : m + 1, l], pltpu.roll(x, tile - 1, 0))
                south = lambda: f[m, lat, :, l]
                north = lambda: f[m, lat + 2, :, l]
                keep(m, c, l, vc * x + va * pick(zspan[c], west, east) + vb * pick(mspan[c], south, north))

    def stage(q, c, l, v):
        hi = v.astype(jnp.bfloat16)
        lhs[q, l] = hi
        lhs[q, width + c * LANES : width + (c + 1) * LANES] = (v - hi.astype(jnp.float32)).astype(jnp.bfloat16)

    chunk = 2 * LANES

    def product(l, high=None):
        left_side = jnp.concatenate([lhs[:high], lhs[:high, :width]], axis=1)
        return jnp.dot(left_side, rk[:, l], preferred_element_type=jnp.float32)

    def members_part(g):
        for c in halo_copies(0, g):
            c.wait_recv()

        @pl.loop(0, block, unroll=True)
        def _(i):
            lat = g * block + i
            r = pl.ds(pl.multiple_of(lat * tile, 8), tile)

            def keep(m, c, l, v):
                gm[m, r, l] = v
                stage(pl.ds(pl.multiple_of((i * count + m) * tile, 16), tile), c, l, v)

            advect(0, f0, lat, count, keep)

        for c in range(0, width, chunk):
            l = slice(c, c + chunk)
            t = product(l)
            for i in range(block):
                for m in range(count):
                    k = (i * count + m) * tile
                    f1[m, g * block + i + 1, :, l] = t[k : k + tile]

    def difference_part():
        @pl.loop(0, blocks)
        def _(g):
            for c in halo_copies(2, g):
                c.wait_recv()

            @pl.loop(0, block, unroll=True)
            def _(i):
                lat = g * block + i
                r = pl.ds(pl.multiple_of(lat * tile, 16), tile)

                def keep(m, c, l, v):
                    gbuf[r, l] = v
                    stage(r, c, l, v)

                advect(2, fd, lat, 1, keep)

        for c in range(0, width, chunk):
            l = slice(c, c + chunk)
            td[:, l] = product(l, cells)

    def join():
        @pl.loop(0, blocks)
        def _(g):
            @pl.loop(0, block, unroll=True)
            def _(i):
                lat = g * block + i
                r = pl.ds(pl.multiple_of(lat * tile, 16), tile)
                acc = [None] * count
                for c in range(cols):
                    l = slice(c * LANES, (c + 1) * LANES)
                    d = gbuf[r, l]
                    for m in range(count):
                        v = gm[m, r, l] + d
                        acc[m] = v * v if c == 0 else acc[m] + v * v
                e = [jnp.broadcast_to(jnp.sum(a, axis=1, keepdims=True) * (0.05 / bins), (tile, LANES)) for a in acc]
                for c in range(cols):
                    l = slice(c * LANES, (c + 1) * LANES)
                    d, w, t = gbuf[r, l], tw[r, l], td[r, l]
                    for m in range(count):
                        f1[m, lat + 1, :, l] = (gm[m, r, l] + d) * (w - e[m]) + (f1[m, lat + 1, :, l] + t)
                keep_edges(1, f1, lat)
            for c in halo_copies(1, g):
                c.start()

    def last_substep():
        @pl.loop(0, blocks)
        def _(g):
            for c in halo_copies(1, g):
                c.wait_recv()

            @pl.loop(0, block, unroll=True)
            def _(i):
                lat = g * block + i
                acc = [None] * count

                def keep(m, c, l, v):
                    acc[m] = v * v if c == 0 else acc[m] + v * v
                    q = pl.ds(pl.multiple_of((i * count + m) * tile, 16), tile)
                    gbuf[q, l] = v
                    stage(q, c, l, v)

                advect(1, f1, lat, count, keep)
                for m in range(count):
                    q = pl.ds(pl.multiple_of((i * count + m) * tile, 16), tile)
                    e = jnp.sum(acc[m], axis=1, keepdims=True) * (0.05 / bins)
                    ebuf[q, :] = jnp.broadcast_to(e, (tile, LANES))

            for c in range(0, width, chunk):
                l = slice(c, c + chunk)
                t = product(l)
                for i in range(block):
                    lat = g * block + i
                    w = tw[pl.ds(pl.multiple_of(lat * tile, 8), tile), l]
                    for m in range(count):
                        k = (i * count + m) * tile
                        e = ebuf[k : k + tile, :]
                        e = jnp.concatenate([e] * (chunk // LANES), axis=1)
                        to_out(m, lat, l, gbuf[k : k + tile, l] * (w - e) + t[k : k + tile])
            out_copy(g).start()

    work = [lambda g=g: members_part(g) for g in range(blocks)]
    for g in range(blocks):
        recentre(0, g)
    for s in range(1, bits):
        for h in (0, 1):
            take(h, s - 1)
            rs_copy(h, s).start()
        if s == 1:
            prepare()
        if work:
            work.pop(0)()
    for h in (0, 1):
        take(h, bits - 1)
        ag_copy(h, bits - 1).start()
    for s in reversed(range(bits - 1)):
        if work:
            work.pop(0)()
        for h in (0, 1):
            ag_arrival(h, s + 1).wait_recv()
            ag_copy(h, s).start()
    for h in (0, 1):
        recentre(2, 2 * h + bit(ways[h][0]))
    for w in work:
        w()
    for h in (0, 1):
        ag_arrival(h, 0).wait_recv()
        recentre(2, 2 * h + 1 - bit(ways[h][0]))

    def out_copy(g):
        r = pl.ds(pl.multiple_of(g * block * tile, 8), block * tile)
        return pltpu.make_async_copy(mv.at[:, r], out_hbm.at[:, r], out_sem.at[g])

    def to_out(m, lat, l, v):
        stop = min(l.stop, bins)
        mv[m, pl.ds(pl.multiple_of(lat * tile, 8), tile), l.start : stop] = v[:, : stop - l.start]

    difference_part()
    join()
    last_substep()

    for h in (0, 1):
        for s in range(bits):
            rs_copy(h, s).wait_send()
            ag_copy(h, s).wait_send()

    @pl.loop(0, blocks)
    def _(g):
        for sub in range(3):
            for c in halo_copies(sub, g):
                c.wait_send()
        out_copy(g).wait()


def shards(members, control, sea_mask, depth_class, wind_dir, growth, rate_kernel):
    count, tile, rows_lat, bins = members.shape
    n, lons = lax.axis_size("mem"), lax.axis_size("lon")
    cells = rows_lat * tile
    width = round_up(bins, 2 * LANES)
    bits = n.bit_length() - 1
    assert n == 1 << bits and cells % (4 * n) == 0
    block = 3 if rows_lat % 3 == 0 else 1
    blocks = rows_lat // block
    tab, wind, cs, sn = constants(bins, width)

    m = members.transpose(0, 2, 1, 3).reshape(count, cells, bins)
    c = control.transpose(1, 0, 2).reshape(cells, control.shape[2])
    spread = growth[None]

    f32, bf16 = jnp.float32, jnp.bfloat16
    vmem = pl.BlockSpec(memory_space=pltpu.VMEM)
    hbm = pl.BlockSpec(memory_space=pl.ANY)
    field = pltpu.VMEM((count, rows_lat + 2, tile, width), f32)
    table = pltpu.VMEM((cells, width), f32)
    rows = block * count * tile
    assert rows >= cells
    out = pl.pallas_call(
        functools.partial(
            kernel, n, lons, count, rows_lat, tile, bins, width, spans(cs), spans(sn), count * n,
        ),
        out_shape=jax.ShapeDtypeStruct((count, cells, bins), f32),
        in_specs=[hbm, hbm, hbm] + [vmem] * 6,
        out_specs=hbm,
        scratch_shapes=[
            pltpu.VMEM((count, cells, bins), f32),
            pltpu.VMEM((cells, control.shape[2]), f32),
            pltpu.VMEM((bins, bins), f32),
            pltpu.VMEM((cells, bins), f32),
            pltpu.VMEM((cells, bins), f32),
            pltpu.VMEM((2, cells // 2, bins), f32),
            pltpu.VMEM((cells, bins), f32),
            pltpu.VMEM((cells, SLOTS), f32),
            field, field, table, table, table, table,
            pltpu.VMEM((3 * width, width), bf16),
            pltpu.VMEM((rows, 2 * width), bf16),
            pltpu.VMEM((rows, width), f32),
            pltpu.VMEM((rows, LANES), f32),
            pltpu.VMEM((1, rows_lat + 2, tile, width), f32),
            pltpu.VMEM((count, cells, width), f32),
            table,
            pltpu.VMEM((3, 2, rows_lat, count, width), f32),
            pltpu.VMEM((3, 2, rows_lat, count, width), f32),
            pltpu.SemaphoreType.DMA((4,)),
            pltpu.SemaphoreType.DMA((2,)),
            pltpu.SemaphoreType.DMA((blocks,)),
            pltpu.SemaphoreType.DMA((2, bits)),
            pltpu.SemaphoreType.DMA((2, bits)),
            pltpu.SemaphoreType.DMA((2, bits)),
            pltpu.SemaphoreType.DMA((2, bits)),
            pltpu.SemaphoreType.DMA((3, 2, blocks)),
            pltpu.SemaphoreType.DMA((3, 2, blocks)),
        ],
        compiler_params=pltpu.CompilerParams(
            collective_id=0, has_side_effects=True, vmem_limit_bytes=58 * 1024 * 1024
        ),
    )(m, c, rate_kernel, sea_mask.T, depth_class.T, wind_dir.T, jnp.asarray(tab), jnp.asarray(wind), spread)
    return out.reshape(count, rows_lat, tile, bins).transpose(0, 2, 1, 3)


def solution(mesh):
    return jax.shard_map(
        shards,
        mesh=mesh,
        in_specs=(
            P("mem", "lon", None, None),
            P("lon", None, "mem"),
            P("lon", None),
            P("lon", None),
            P("lon", None),
            P(),
            P(),
        ),
        out_specs=P("mem", "lon", None, None),
        check_vma=False,
    )
```
